32 devices in a mesh: pos: 4 (over x, core), filt: 4 (over z), layer: 2 (over y).
Axes of the slice: x: 2, y: 2, z: 4, core: 2. Of those that a mesh axis runs over, the one named last changes fastest.
Arguments:
- activations: float32 [128, 1024, 128], P('pos', ('layer', 'filt')), may hold values from -6 to 6
- filters: float32 [9, 1024, 1024], P(None, ('layer', 'pos'), 'filt'), may hold values from -0.0625 to 0.0625
Outputs:
- rectified: float32 [128, 1024, 128], P('pos', ('filt', 'layer'))
The draws below stay inside these ranges and needn't reach their ends.
All inputs are finite; a program needn't handle non-finite values.
Results may differ from the reference program's by a relative error of at most 0.0001.
Values sent between devices are 32-bit elements; how exact they have to be, the bound alone decides.
No kernel may reach another device: no remote copies, remote signals or barrier semaphores. Data moves between devices by JAX's collectives and lax.ppermute only.
A program may use at most 128 MiB of HBM per device.

```python
import jax
import jax.numpy as jnp
from jax import lax

CIN = 1024
COUT = 1024
COLS = 128
HEIGHT = 128


def level_of(key, extent, shards, smallest, high):
    factor_of = 1.0
    for position, shards_of in shards:
        heights = jax.random.uniform(jax.random.fold_in(jax.random.fold_in(key, 6), position), (shards_of,), jnp.float32, smallest / len(shards), high / len(shards))
        factor_of = factor_of * jnp.repeat(jnp.exp(heights), extent[position] // shards_of).reshape((-1,) + (1,) * (len(extent) - 1 - position))
    return factor_of


def noise(stream_key, shape, width, most, cuts=(), kind=jnp.bfloat16):
    level = level_of(stream_key, shape, cuts, -0.22, 0.18) if cuts else 1.0
    array = jax.random.normal(stream_key, shape, jnp.float32) * width * level
    return jnp.minimum(jnp.maximum(array, -most), most).astype(kind)


def setup_inputs(seed: int = 0) -> dict:
    key_of = jax.random.split(jax.random.key(seed), 3)
    return {
        "activations": noise(key_of[0], (HEIGHT, CIN, COLS), 1.0, 6.0, ((0, 4), (1, 8)), jnp.float32),
        "filters": noise(key_of[1], (9, CIN, COUT), (9 * CIN) ** -0.5, 0.0625, ((1, 8), (2, 4)), jnp.float32),
    }


def reference(activations, filters):
    height = activations.shape[0]
    across = activations.shape[2]
    padded = jnp.pad(activations, ((1, 1), (0, 0), (1, 1)))
    summed = jnp.zeros((height, filters.shape[2], across), jnp.float32)
    for tap_index in range(9):
        row_shift, col_shift = divmod(tap_index, 3)
        window = padded[row_shift:row_shift + height, :, col_shift:col_shift + across]
        summed = summed + jnp.einsum('ric,io->roc', window, filters[tap_index], precision=lax.Precision.HIGHEST)
    return jnp.maximum(summed, 0.0)
```

```python
import functools

import jax
import jax.numpy as jnp
from jax import lax
from jax.experimental import pallas as pl
from jax.experimental.pallas import tpu as pltpu
from jax.sharding import PartitionSpec as P

VMEM_BYTES = 48 << 20
APART = False
SHARES = (5, 5, 4, 2)
DEPTHS = (2, 2, 2)
FACTOR = 1.0
EFFORT = 0.0


def split(value):
    high = value.astype(jnp.bfloat16)
    low = (value - high.astype(jnp.float32)).astype(jnp.bfloat16)
    return high, low


def prepare_kernel(place_ref, *refs):
    pieces, (high_ref, low_ref) = refs[:-2], refs[-2:]
    for index, piece in enumerate(pieces):
        depth, wide = piece.shape[1:]
        high, low = split(piece[0].T)
        half = wide // 2
        columns = slice(None)
        if len(pieces) > 1:
            columns = pl.ds(pl.multiple_of(place_ref[1 + index] * depth, depth), depth)
        for side in range(2):
            rows = place_ref[0] * half if side else (1 - place_ref[0]) * half
            rows = pl.ds(pl.multiple_of(rows, half), half)
            source = slice(side * half, (side + 1) * half)
            high_ref[0, rows, columns] = high[source]
            low_ref[0, rows, columns] = low[source]


def prepare(pieces, place):
    wide = pieces[0].shape[2]
    depth = sum(piece.shape[1] for piece in pieces)
    shape = jax.ShapeDtypeStruct((3, 3 * wide, depth), jnp.bfloat16)
    block = pl.BlockSpec((1, wide, depth), lambda t, s: (t // 3, t % 3, 0))
    return pl.pallas_call(
        prepare_kernel,
        out_shape=(shape, shape),
        grid_spec=pltpu.PrefetchScalarGridSpec(
            num_scalar_prefetch=1,
            grid=(9,),
            in_specs=[pl.BlockSpec((1,) + piece.shape[1:], lambda t, s: (t, 0, 0)) for piece in pieces],
            out_specs=(block, block),
        ),
        compiler_params=pltpu.CompilerParams(vmem_limit_bytes=VMEM_BYTES),
        cost_estimate=pl.CostEstimate(flops=1000 + int(EFFORT * 1e9), bytes_accessed=1000, transcendentals=0),
    )(place, *pieces)


def conv_kernel(sources, ahead, pairs, start, end, parts, place_ref, *refs):
    size = 1 + max(index for group in sources + ahead for index in group)
    arrays, refs = refs[:size], refs[size:]
    before, high_w, low_w = refs[:3]
    results, tail, high_x, low_x = refs[3 : 3 + len(parts)], refs[3 + len(parts)], *refs[4 + len(parts) :]
    channels, across = arrays[0].shape[1:]
    wide = high_w.shape[1] // 3
    half = wide // 2

    def put(side, row, slot, value):
        high, low = split(value)
        rows = pl.ds(pl.multiple_of(place_ref[slot] * channels, channels), channels)
        high_x[side, row, rows, :] = high
        low_x[side, row, rows, :] = low

    def put_rows(groups, first, many):
        for slot, group in enumerate(groups):
            for row in range(many):
                for side in range(2):
                    from_row = arrays[group[0]].shape[0] - 1 - row if side else row
                    value = arrays[group[0]][from_row]
                    for index in group[1:]:
                        value = value + arrays[index][from_row]
                    put(side, first + row, slot, value)

    if start == "halo":
        for side in range(2):
            for slot in range(len(sources)):
                put(side, 0, slot, before[side, slot])
    elif start == "tail":
        for side in range(2):
            for row in range(2):
                high_x[side, row] = before[0, side, row]
                low_x[side, row] = before[1, side, row]
    base = STARTS[start]
    total = base + pairs
    put_rows(sources, base, pairs)
    for side in range(2):
        for row in range(2):
            tail[0, side, row] = high_x[side, total - 2 + row]
            tail[1, side, row] = low_x[side, total - 2 + row]
    if end == "meet":
        for side in range(2):
            high_x[side, total] = high_x[1 - side, total - 1]
            low_x[side, total] = low_x[1 - side, total - 1]
    elif end == "ahead":
        put_rows(ahead, total, 2)
    outs = total + ENDS[end] - 2
    taken = half * len(parts)
    lane = lax.broadcasted_iota(jnp.int32, (taken, across), 1)

    def rows_of(ref, a):
        if len(parts) == 2:
            return ref[a]
        return jnp.concatenate([ref[a, pl.ds(b * wide + parts[0] * half, half)] for b in range(3)], axis=0)

    def step(q, carry):
        total_sum = None
        for a in range(3):
            high = jnp.concatenate([high_x[0, q + a], high_x[1, q + 2 - a]], axis=1)
            low = jnp.concatenate([low_x[0, q + a], low_x[1, q + 2 - a]], axis=1)
            dot = functools.partial(jnp.dot, preferred_element_type=jnp.float32)
            high_rows, low_rows = rows_of(high_w, a), rows_of(low_w, a)
            part = dot(high_rows, high) + dot(high_rows, low) + dot(low_rows, high)
            total_sum = part if total_sum is None else total_sum + part
        for side in range(2):
            lanes = slice(side * across, (side + 1) * across)
            left = pltpu.roll(total_sum[:taken, lanes], 1, 1)
            right = pltpu.roll(total_sum[2 * taken :, lanes], across - 1, 1)
            result = (
                total_sum[taken : 2 * taken, lanes]
                + jnp.where(lane == 0, 0.0, left)
                + jnp.where(lane == across - 1, 0.0, right)
            )
            row = q if side == 0 else outs - 1 - q
            for index, ref in enumerate(results):
                ref[side, row] = result[index * half : (index + 1) * half]
        return carry

    lax.fori_loop(0, outs, step, 0)


STARTS = {"none": 0, "halo": 1, "tail": 2}
ENDS = {"none": 0, "meet": 1, "ahead": 2}


def conv(place, groups, before, weights, pairs, start, end, ahead, parts):
    arrays, numbers = [], []
    for group in list(groups) + list(ahead):
        numbers.append(tuple(range(len(arrays), len(arrays) + len(group))))
        arrays += group
    sources, ahead = tuple(numbers[: len(groups)]), tuple(numbers[len(groups) :])
    channels, across = arrays[0].shape[1:]
    depth = channels * len(groups)
    wide = weights[0].shape[1] // 3
    rows = STARTS[start] + pairs + ENDS[end]
    outs = rows - 2
    result = jax.ShapeDtypeStruct((2, outs, wide // 2, across), jnp.float32)
    tail = jax.ShapeDtypeStruct((2, 2, 2, depth, across), jnp.bfloat16)
    vmem = pl.BlockSpec(memory_space=pltpu.VMEM)
    flops = 2 * 2 * outs * across * 9 * depth * wide * 3 * len(parts) // 2
    return pl.pallas_call(
        functools.partial(conv_kernel, sources, ahead, pairs, start, end, parts),
        out_shape=(result,) * len(parts) + (tail,),
        in_specs=[pl.BlockSpec(memory_space=pltpu.SMEM)] + [vmem] * (len(arrays) + 3),
        out_specs=(vmem,) * (len(parts) + 1),
        scratch_shapes=[
            pltpu.VMEM((2, rows, depth, across), jnp.bfloat16),
            pltpu.VMEM((2, rows, depth, across), jnp.bfloat16),
        ],
        compiler_params=pltpu.CompilerParams(vmem_limit_bytes=VMEM_BYTES),
        cost_estimate=pl.CostEstimate(flops=1000 + int(flops * FACTOR), bytes_accessed=1000, transcendentals=0),
    )(place, *arrays, before, *weights)


class Cell:
    def __init__(self, value):
        self.value = value


def after(value, cells):
    cells = [cell for cell in cells if cell is not None]
    if not cells:
        return value
    value, *others = lax.optimization_barrier((value, *(cell.value for cell in cells)))
    for cell, other in zip(cells, others):
        cell.value = other
    return value


class Lane:
    def __init__(self, axis, most=2):
        self.axis, self.most, self.sent = axis, most, []

    def send(self, value, pairs, *cells):
        held = self.sent[-self.most] if len(self.sent) >= self.most else None
        cell = Cell(lax.ppermute(after(value, (held,) + cells), self.axis, pairs))
        self.sent.append(cell)
        return cell


def edges(count, step, parity, ends):
    moves = []
    for low in range(parity, count - 1, 2):
        if low >= step and (ends or low + 1 < count - 1):
            moves.append((low, low + 1))
        if low + 1 <= count - 1 - step and (ends or low > 0):
            moves.append((low + 1, low))
    return moves


def gathered(piece, lane, cells=()):
    count = lax.axis_size("pos")
    pieces = {0: Cell(piece)}
    bit = count // 2
    while bit:
        swap = [(i, i ^ bit) for i in range(count)]
        pieces.update({key ^ bit: lane.send(cell.value, swap, *cells) for key, cell in list(pieces.items())})
        bit //= 2
    return pieces


def chunk_sizes(half):
    total = sum(SHARES)
    return [half * share // total for share in SHARES] if half % total == 0 else [half]


ORDER = (('E00',), ('O00',), ('E10',), ('O01',), ('E01',), ('O10',), ('E02',), ('O11',), ('E12', 'E01'), ('E11',), ('O20',), ('H', 'O20'), ('P',), ('K0', 'E11'), ('E20', 'X3'), ('O21',), ('E21',), ('K1',), ('E30',), ('O30',), ('E22',), ('O31', 'E20'), ('E31',), ('K2', 'Y0', 'E22'), ('E32',), ('K3',))


def body(activations, filters):
    count = lax.axis_size("filt")
    me = lax.axis_index("filt")
    layer = lax.axis_index("layer")
    position, positions = lax.axis_index("pos"), lax.axis_size("pos")
    height, channels, across = activations.shape
    half = height // 2
    apart = APART and count >= 4 and half % sum(SHARES) == 0
    forward = [(i, i + 1) for i in range(positions - 1)]
    backward = [(i + 1, i) for i, _ in forward]
    swap = [(0, 1), (1, 0)]

    sizes = chunk_sizes(half)
    starts = [sum(sizes[:i]) for i in range(len(sizes))]
    chunks = [
        jnp.concatenate([activations[s : s + m], activations[height - s - m : height - s]], axis=0)
        for s, m in zip(starts, sizes)
    ]
    lanes = {"E": Lane("filt", DEPTHS[0]), "O": Lane("filt", DEPTHS[1]), "W": Lane("filt"), "Y": Lane("layer", DEPTHS[2])}
    lanes["X"] = Lane("pos", 99)
    by_swaps = positions & (positions - 1) == 0 and filters.shape[1] % 128 == 0
    turn = 1 - 2 * (me % 2)
    place = jnp.mod(me + turn * jnp.arange(count), count).astype(jnp.int32)
    order = layer.astype(jnp.int32).reshape(1)
    if by_swaps:
        keys = gathered_keys(positions)
        order = jnp.concatenate([order, jnp.stack([position ^ key for key in keys]).astype(jnp.int32)])
    cells = {}

    def spread(name, piece, waits=()):
        if not by_swaps:
            cells[name + "0"] = Cell(lax.all_gather(piece, "pos", axis=1, tiled=True))
            return
        pieces = gathered(piece, lanes["X"], waits)
        cells.update({name + str(index): pieces[key] for index, key in enumerate(keys)})

    def prepared(name):
        pieces = [cells[key].value for key in sorted(cells) if key[0] == name]
        return [Cell(array) for array in prepare(pieces, order)]

    def move(word, waits):
        kind, index, step = word[0], int(word[1]), int(word[2])
        ends = index > 0 or not apart
        source = Cell(chunks[index]) if step == 0 else cells.get("OE"["EO".index(kind)] + f"{index}{step - 1}")
        moves = edges(count, step, "EO".index(kind), ends)
        if moves and source is not None:
            lane = "W" if kind == "E" and not ends else kind
            cells[word] = lanes[lane].send(source.value, moves, *waits)

    def groups(index):
        result = [[chunks[index]]]
        for slot in range(1, count):
            words = [f"E{index}{slot - 1}"] + ([f"O{index}{count - 1 - slot}"] if slot >= 2 else [])
            result.append([cells[word].value for word in words if word in cells])
        return result

    def halo():
        parts = groups(0)
        above, below = (
            jnp.stack([sum(array[row] for array in part) for part in parts]) for row in (2 * sizes[0] - 1, 0)
        )
        return Cell(jnp.stack([lax.ppermute(above, "pos", forward), lax.ppermute(below, "pos", backward)]))

    tails = {}

    def compute(kind, index, waits, parts=(0, 1)):
        first, last = index == 0, index == len(chunks) - 1
        if first:
            before, start = cells["H"].value, "halo"
        elif index == 1 and apart:
            before, start = order, "none"
        else:
            before, start = tails[index - 1], "tail"
        end, ahead = "meet" if last else "none", ()
        if first and apart:
            end, ahead = "ahead", groups(1)
        weights = [cell.value for cell in (own_weights if kind == "K" else end_weights)]
        before = after(before, waits)
        *results, tails[index] = conv(
            place, groups(index), before, weights, sizes[index], start, end, ahead, parts
        )
        if 1 in parts:
            cells[f"{kind}{index}"] = Cell(results[-1])
        if 0 in parts:
            cells[("Y" if kind == "K" else "Z") + str(index)] = lanes["Y"].send(results[0], swap)

    def total(kind, index):
        other = cells[("Y" if kind == "K" else "Z") + str(index)]
        return jnp.maximum(cells[f"{kind}{index}"].value + other.value, 0.0)

    first = Cell(chunks[0])
    spread("X", after(filters, [first]))
    chunks[0] = first.value
    if len(chunks) > 1 and count == 4:
        plan = ORDER
    else:
        plan = [("W",), ("P",), ("Q",)]
        for index in range(len(chunks)):
            for step in range(count - 1):
                plan += [(f"E{index}{step}",)] + ([(f"O{index}{step}",)] if step < count - 2 else [])
        plan += [("H",)] + [(f"K{index}",) for index in range(len(chunks))] + [("L0",), ("S",)]
    for word, *names in plan:
        kind = word[0]
        waits = [cells[name] for name in names if name in cells]
        if kind in "EO":
            move(word, waits)
        elif kind == "H":
            cells["H"] = halo()
        elif kind == "P":
            own_weights = prepared("X")
            cells["P"] = own_weights[0]
        elif kind == "K":
            compute(kind, int(word[1]), waits)
        elif kind in "AB":
            compute("K", int(word[1]), waits, ("AB".index(kind),))
        elif not apart:
            continue
        elif kind == "L":
            compute(kind, int(word[1]), waits)
        elif kind == "W":
            cells["W"] = lanes["W"].send(filters, [(0, 1), (count - 1, count - 2)], *waits)
            spread("V", cells["W"].value, [cells[name] for name in ("X1",) if name in cells])
        elif kind == "Q":
            end_weights = prepared("V")
            cells["Q"] = end_weights[0]
        elif kind == "S":
            result = after(total("L", 0), waits)
            cells["S"] = lanes["E"].send(result, [(1, 0), (count - 2, count - 1)])
    blocks = [total("K", index) for index in range(len(chunks))]
    if apart:
        at_end = (me == 0) | (me == count - 1)
        blocks[0] = jnp.where(at_end, cells["S"].value, blocks[0])
    return jnp.concatenate([block[0] for block in blocks] + [block[1] for block in reversed(blocks)], axis=0)


def gathered_keys(positions):
    keys = [0]
    bit = positions // 2
    while bit:
        keys += [key ^ bit for key in keys]
        bit //= 2
    return keys


def solution(mesh):
    in_specs = (P("pos", ("layer", "filt"), None), P(None, ("layer", "pos"), "filt"))
    out_specs = P("pos", ("filt", "layer"), None)
    return jax.shard_map(body, mesh=mesh, in_specs=in_specs, out_specs=out_specs, check_vma=False)
```

```python
import functools

import jax
import jax.numpy as jnp
from jax import lax
from jax.experimental import pallas as pl
from jax.experimental.pallas import tpu as pltpu
from jax.sharding import PartitionSpec as P

VMEM_BYTES = 48 << 20
SHARES = (5, 5, 4, 2)
DEPTHS = (3, 3, 2)
FACTOR = 0.0
EFFORT = 0.0


def split(value):
    high = value.astype(jnp.bfloat16)
    low = (value - high.astype(jnp.float32)).astype(jnp.bfloat16)
    return high, low


def prepare_kernel(late, place_ref, *refs):
    outs = 4 if late else 2
    pieces, outputs = refs[:-outs], refs[-outs:]
    last = outputs[0].shape[1]
    for index, piece in enumerate(pieces):
        depth, wide = piece.shape[1:]
        half = wide // 2
        pair = split(piece[0].T)

        def store(targets, columns):
            for side in range(2):
                rows = place_ref[0] * half if side else (1 - place_ref[0]) * half
                rows = pl.ds(pl.multiple_of(rows, half), half)
                for ref, value in zip(targets, pair):
                    value = value[side * half : (side + 1) * half]
                    ref[rows, columns] = value

        if len(pieces) == 1:
            store(outputs, slice(None))
        elif not late:
            store(outputs, pl.ds(pl.multiple_of(place_ref[1 + index] * depth, depth), depth))
        else:
            column = place_ref[1 + index] * depth

            @pl.when(column < last)
            def _():
                store(outputs[:2], pl.ds(pl.multiple_of(column, depth), depth))

            @pl.when(column >= last)
            def _():
                store(outputs[2:], slice(None))


def prepare(pieces, place, late):
    channels, wide = pieces[0].shape[1:]
    depth = channels * len(pieces)
    early = depth - channels if late else depth
    shapes = [jax.ShapeDtypeStruct((3 * wide, 3 * early), jnp.bfloat16)] * 2
    blocks = [pl.BlockSpec((wide, early), lambda t, s: (t % 3, t // 3))] * 2
    if late:
        shapes += [jax.ShapeDtypeStruct((3 * wide, 3 * channels), jnp.bfloat16)] * 2
        blocks += [pl.BlockSpec((wide, channels), lambda t, s: (t % 3, t // 3))] * 2
    return pl.pallas_call(
        functools.partial(prepare_kernel, late),
        out_shape=tuple(shapes),
        grid_spec=pltpu.PrefetchScalarGridSpec(
            num_scalar_prefetch=1,
            grid=(9,),
            in_specs=[pl.BlockSpec((1,) + piece.shape[1:], lambda t, s: (t, 0, 0)) for piece in pieces],
            out_specs=tuple(blocks),
        ),
        compiler_params=pltpu.CompilerParams(vmem_limit_bytes=VMEM_BYTES),
        cost_estimate=pl.CostEstimate(flops=1000 + int(EFFORT * 1e9), bytes_accessed=1000, transcendentals=0),
    )(place, *pieces)


def conv_kernel(sources, pairs, first, last, added, place_ref, *refs):
    size = 1 + max(index for group in sources for index in group)
    arrays, refs = refs[:size], refs[size:]
    before, high_w, low_w = refs[:3]
    sums, refs = refs[3 : 3 + 2 * added], refs[3 + 2 * added :]
    results, tail, high_x, low_x = refs[:2], *refs[2:]
    channels, across = arrays[0].shape[1:]
    wide = high_w.shape[0] // 3
    half = wide // 2
    base = 1 if first else 2

    def put(side, row, slot, value):
        high, low = split(value)
        rows = pl.ds(pl.multiple_of(place_ref[slot] * channels, channels), channels)
        high_x[side, row, rows, :] = high
        low_x[side, row, rows, :] = low

    if first:
        for side in range(2):
            for slot in range(len(sources)):
                put(side, 0, slot, before[side, slot])
    else:
        for side in range(2):
            for row in range(2):
                high_x[side, row] = before[0, side, row]
                low_x[side, row] = before[1, side, row]
    for slot, group in enumerate(sources):
        for row in range(pairs):
            for side in range(2):
                from_row = 2 * pairs - 1 - row if side else row
                value = arrays[group[0]][from_row]
                for index in group[1:]:
                    value = value + arrays[index][from_row]
                put(side, base + row, slot, value)
    total = base + pairs
    for side in range(2):
        for row in range(2):
            tail[0, side, row] = high_x[side, total - 2 + row]
            tail[1, side, row] = low_x[side, total - 2 + row]
    if last:
        for side in range(2):
            high_x[side, total] = high_x[1 - side, total - 1]
            low_x[side, total] = low_x[1 - side, total - 1]
        total += 1
    outs = total - 2
    lane = lax.broadcasted_iota(jnp.int32, (wide, across), 1)
    dot = functools.partial(jnp.dot, preferred_element_type=jnp.float32)

    def step(q, carry):
        taps = [
            [jnp.concatenate([ref[0, q + a], ref[1, q + 2 - a]], axis=1) for a in range(3)] for ref in (high_x, low_x)
        ]
        high, low = taps
        rows = jnp.concatenate([high_w[...], high_w[...], low_w[...]], axis=1)
        total_sum = dot(rows, jnp.concatenate(high + low + high, axis=0))
        for side in range(2):
            lanes = slice(side * across, (side + 1) * across)
            left = pltpu.roll(total_sum[:wide, lanes], 1, 1)
            right = pltpu.roll(total_sum[2 * wide :, lanes], across - 1, 1)
            result = (
                total_sum[wide : 2 * wide, lanes]
                + jnp.where(lane == 0, 0.0, left)
                + jnp.where(lane == across - 1, 0.0, right)
            )
            row = q if side == 0 else outs - 1 - q
            for index, ref in enumerate(results):
                value = result[index * half : (index + 1) * half]
                ref[side, row] = value + sums[index][side, row] if added else value
        return carry

    lax.fori_loop(0, outs, step, 0)


def conv(place, groups, before, weights, pairs, first, last, sums=()):
    arrays, numbers = [], []
    for group in groups:
        numbers.append(tuple(range(len(arrays), len(arrays) + len(group))))
        arrays += group
    channels, across = arrays[0].shape[1:]
    depth = channels * len(groups)
    wide = weights[0].shape[0] // 3
    rows = (1 if first else 2) + pairs + (1 if last else 0)
    outs = rows - 2
    result = jax.ShapeDtypeStruct((2, outs, wide // 2, across), jnp.float32)
    tail = jax.ShapeDtypeStruct((2, 2, 2, depth, across), jnp.bfloat16)
    vmem = pl.BlockSpec(memory_space=pltpu.VMEM)
    flops = 2 * 2 * outs * across * 9 * depth * wide * 3
    return pl.pallas_call(
        functools.partial(conv_kernel, tuple(numbers), pairs, first, last, bool(sums)),
        out_shape=(result, result, tail),
        in_specs=[pl.BlockSpec(memory_space=pltpu.SMEM)] + [vmem] * (len(arrays) + 3 + len(sums)),
        out_specs=(vmem, vmem, vmem),
        scratch_shapes=[
            pltpu.VMEM((2, rows, depth, across), jnp.bfloat16),
            pltpu.VMEM((2, rows, depth, across), jnp.bfloat16),
        ],
        compiler_params=pltpu.CompilerParams(vmem_limit_bytes=VMEM_BYTES),
        cost_estimate=pl.CostEstimate(flops=1000 + int(flops * FACTOR), bytes_accessed=1000, transcendentals=0),
    )(place, *arrays, before, *weights, *sums)


class Cell:
    def __init__(self, value):
        self.value = value


def after(value, cells):
    cells = [cell for cell in cells if cell is not None]
    if not cells:
        return value
    value, *others = lax.optimization_barrier((value, *(cell.value for cell in cells)))
    for cell, other in zip(cells, others):
        cell.value = other
    return value


class Lane:
    def __init__(self, axis, most=2):
        self.axis, self.most, self.sent = axis, most, []

    def send(self, value, pairs, *cells):
        held = self.sent[-self.most] if len(self.sent) >= self.most else None
        cell = Cell(lax.ppermute(after(value, (held,) + cells), self.axis, pairs))
        self.sent.append(cell)
        return cell


def edges(count, step, parity):
    moves = []
    for low in range(parity, count - 1, 2):
        if low >= step:
            moves.append((low, low + 1))
        if low + 1 <= count - 1 - step:
            moves.append((low + 1, low))
    return moves


def gathered_keys(positions):
    keys = [0]
    bit = positions // 2
    while bit:
        keys += [key ^ bit for key in keys]
        bit //= 2
    return keys


def gathered(piece, lane):
    count = lax.axis_size("pos")
    pieces = {0: Cell(piece)}
    bit = count // 2
    while bit:
        swap = [(i, i ^ bit) for i in range(count)]
        pieces.update({key ^ bit: lane.send(cell.value, swap) for key, cell in list(pieces.items())})
        bit //= 2
    return [pieces[key] for key in gathered_keys(count)]


def chunk_sizes(half):
    total = sum(SHARES)
    return [half * share // total for share in SHARES] if half % total == 0 else [half]


ORDER = (
    ("E00",), ("O00",), ("E10",), ("O01",), ("E01",), ("O10",), ("E02",), ("O11",), ("E11",), ("O20", "X2"),
    ("P", "X3"), ("E20",), ("O21",), ("H",), ("E12", "H"), ("O30",), ("A0",), ("E21", "A0"), ("E30", "E12"), ("O31",),
    ("A1",), ("G",), ("E22", "A1"), ("B0", "A0"), ("E31",), ("A2",), ("B1",), ("E32",), ("A3",), ("B2",), ("B3",),
)


def body(activations, filters):
    count, positions = lax.axis_size("filt"), lax.axis_size("pos")
    me, position, layer = lax.axis_index("filt"), lax.axis_index("pos"), lax.axis_index("layer")
    height, channels, across = activations.shape
    half = height // 2
    forward = [(i, i + 1) for i in range(positions - 1)]
    backward = [(i + 1, i) for i, _ in forward]
    swap = [(0, 1), (1, 0)]

    sizes = chunk_sizes(half)
    starts = [sum(sizes[:i]) for i in range(len(sizes))]
    chunks = [
        jnp.concatenate([activations[s : s + m], activations[height - s - m : height - s]], axis=0)
        for s, m in zip(starts, sizes)
    ]
    lanes = {"E": Lane("filt", DEPTHS[0]), "O": Lane("filt", DEPTHS[1]), "Y": Lane("layer", DEPTHS[2])}
    by_swaps = positions & (positions - 1) == 0 and filters.shape[1] % 128 == 0
    late = by_swaps and positions == count == 4 and len(sizes) > 1
    turn = 1 - 2 * (me % 2)
    slots = jnp.arange(count)
    place = (slots if late else jnp.mod(me + turn * slots, count)).astype(jnp.int32)
    order = layer.astype(jnp.int32).reshape(1)
    if by_swaps:
        owners = jnp.stack([position ^ key for key in gathered_keys(positions)])
        owners = jnp.mod(turn * (owners - me), count) if late else owners
        order = jnp.concatenate([order, owners.astype(jnp.int32)])
    cells = {}
    first = Cell(chunks[0])
    held = after(filters, [first])
    chunks[0] = first.value
    if by_swaps:
        pieces = gathered(held, Lane("pos", 99))
    else:
        pieces = [Cell(lax.all_gather(held, "pos", axis=1, tiled=True))]
    cells.update({f"X{index}": cell for index, cell in enumerate(pieces)})

    def move(word, waits):
        kind, index, step = word[0], int(word[1]), int(word[2])
        parity = "EO".index(kind)
        source = Cell(chunks[index]) if step == 0 else cells.get("OE"[parity] + f"{index}{step - 1}")
        moves = edges(count, step, parity)
        if moves and source is not None:
            cells[word] = lanes[kind].send(source.value, moves, *waits)

    def groups(index, taken):
        result = []
        for slot in taken:
            words = [f"E{index}{slot - 1}"] + ([f"O{index}{count - 1 - slot}"] if slot >= 2 else [])
            result.append([cells[word].value for word in words if word in cells] if slot else [chunks[index]])
        return result

    def halo(taken):
        parts = groups(0, taken)
        above, below = (
            jnp.stack([sum(array[row] for array in part) for part in parts]) for row in (2 * sizes[0] - 1, 0)
        )
        return Cell(jnp.stack([lax.ppermute(above, "pos", forward), lax.ppermute(below, "pos", backward)]))

    tails, sums = {}, {}

    def compute(kind, index, waits):
        taken = {"A": range(count - 1), "B": [count - 1], "K": range(count)}[kind]
        begin, end = index == 0, index == len(chunks) - 1
        before = cells["G" if kind == "B" else "H"].value if begin else tails[kind, index - 1]
        weights = [cell.value for cell in prepared[2 * (kind == "B") :][:2]]
        extra = [cell.value for cell in sums[index]] if kind == "B" else ()
        before = after(before, waits)
        send, keep, tails[kind, index] = conv(
            place, groups(index, taken), before, weights, sizes[index], begin, end, extra
        )
        sums[index] = [Cell(send), Cell(keep)]
        cells[f"{kind}{index}"] = sums[index][1]
        if kind != "A":
            cells[f"Y{index}"] = lanes["Y"].send(send, swap)

    if late:
        plan = ORDER
    else:
        plan = [("P",)]
        for index in range(len(chunks)):
            for step in range(count - 1):
                plan += [(f"E{index}{step}",)] + ([(f"O{index}{step}",)] if step < count - 2 else [])
        plan += [("H",)] + [(f"K{index}",) for index in range(len(chunks))]
    for word, *names in plan:
        kind = word[0]
        waits = [cells[name] for name in names if name in cells]
        if kind in "EO":
            move(word, waits)
        elif kind == "P":
            arrays = [cell.value for cell in pieces]
            prepared = [Cell(array) for array in prepare(arrays, order, late)]
            cells["P"] = prepared[0]
        elif kind in "HG":
            cells[kind] = halo([count - 1] if kind == "G" else range(count - 1 if late else count))
        else:
            compute(kind, int(word[1]), waits)
    blocks = [jnp.maximum(sums[index][1].value + cells[f"Y{index}"].value, 0.0) for index in range(len(chunks))]
    return jnp.concatenate([block[0] for block in blocks] + [block[1] for block in reversed(blocks)], axis=0)


def solution(mesh):
    in_specs = (P("pos", ("layer", "filt"), None), P(None, ("layer", "pos"), "filt"))
    out_specs = P("pos", ("filt", "layer"), None)
    return jax.shard_map(body, mesh=mesh, in_specs=in_specs, out_specs=out_specs, check_vma=False)
```

```python
import functools

import jax
import jax.numpy as jnp
from jax import lax
from jax.experimental import pallas as pl
from jax.experimental.pallas import tpu as pltpu
from jax.sharding import PartitionSpec as P

VMEM_BYTES = 48 << 20
SHARES = (5, 5, 4, 2)
DEPTHS = (3, 3, 2)
FACTOR = 0.0
EFFORT = 0.0


def split(value):
    high = value.astype(jnp.bfloat16)
    low = (value - high.astype(jnp.float32)).astype(jnp.bfloat16)
    return high, low


def prepare_kernel(late, place_ref, *refs):
    outs = 4 if late else 2
    pieces, outputs = refs[:-outs], refs[-outs:]
    last = outputs[0].shape[1]
    for index, piece in enumerate(pieces):
        depth, wide = piece.shape[1:]
        half = wide // 2
        pair = [value.T for value in split(piece[0])]

        def store(targets, columns):
            for side in range(2):
                rows = place_ref[0] * half if side else (1 - place_ref[0]) * half
                rows = pl.ds(pl.multiple_of(rows, half), half)
                for ref, value in zip(targets, pair):
                    value = value[side * half : (side + 1) * half]
                    ref[rows, columns] = value

        if len(pieces) == 1:
            store(outputs, slice(None))
        elif not late:
            store(outputs, pl.ds(pl.multiple_of(place_ref[1 + index] * depth, depth), depth))
        else:
            column = place_ref[1 + index] * depth

            @pl.when(column < last)
            def _():
                store(outputs[:2], pl.ds(pl.multiple_of(column, depth), depth))

            @pl.when(column >= last)
            def _():
                store(outputs[2:], slice(None))


def prepare(pieces, place, late):
    channels, wide = pieces[0].shape[1:]
    depth = channels * len(pieces)
    early = depth - channels if late else depth
    shapes = [jax.ShapeDtypeStruct((3 * wide, 3 * early), jnp.bfloat16)] * 2
    blocks = [pl.BlockSpec((wide, early), lambda t, s: (t % 3, t // 3))] * 2
    if late:
        shapes += [jax.ShapeDtypeStruct((3 * wide, 3 * channels), jnp.bfloat16)] * 2
        blocks += [pl.BlockSpec((wide, channels), lambda t, s: (t % 3, t // 3))] * 2
    return pl.pallas_call(
        functools.partial(prepare_kernel, late),
        out_shape=tuple(shapes),
        grid_spec=pltpu.PrefetchScalarGridSpec(
            num_scalar_prefetch=1,
            grid=(9,),
            in_specs=[pl.BlockSpec((1,) + piece.shape[1:], lambda t, s: (t, 0, 0)) for piece in pieces],
            out_specs=tuple(blocks),
        ),
        compiler_params=pltpu.CompilerParams(vmem_limit_bytes=VMEM_BYTES),
        cost_estimate=pl.CostEstimate(flops=1000 + int(EFFORT * 1e9), bytes_accessed=1000, transcendentals=0),
    )(place, *pieces)


def conv_kernel(sources, pairs, first, last, added, place_ref, *refs):
    size = 1 + max(index for group in sources for index in group)
    arrays, refs = refs[:size], refs[size:]
    before, high_w, low_w = refs[:3]
    sums, refs = refs[3 : 3 + 2 * added], refs[3 + 2 * added :]
    results, tail, high_x, low_x = refs[:2], *refs[2:]
    channels, across = arrays[0].shape[1:]
    wide = high_w.shape[0] // 3
    half = wide // 2
    base = 1 if first else 2

    def put(side, row, slot, value):
        high, low = split(value)
        rows = pl.ds(pl.multiple_of(place_ref[slot] * channels, channels), channels)
        high_x[side, row, rows, :] = high
        low_x[side, row, rows, :] = low

    if first:
        for side in range(2):
            for slot in range(len(sources)):
                put(side, 0, slot, before[side, slot])
    else:
        for side in range(2):
            for row in range(2):
                high_x[side, row] = before[0, side, row]
                low_x[side, row] = before[1, side, row]
    for slot, group in enumerate(sources):
        for row in range(pairs):
            for side in range(2):
                from_row = 2 * pairs - 1 - row if side else row
                value = arrays[group[0]][from_row]
                for index in group[1:]:
                    value = value + arrays[index][from_row]
                put(side, base + row, slot, value)
    total = base + pairs
    for side in range(2):
        for row in range(2):
            tail[0, side, row] = high_x[side, total - 2 + row]
            tail[1, side, row] = low_x[side, total - 2 + row]
    if last:
        for side in range(2):
            high_x[side, total] = high_x[1 - side, total - 1]
            low_x[side, total] = low_x[1 - side, total - 1]
        total += 1
    outs = total - 2
    lane = lax.broadcasted_iota(jnp.int32, (wide, across), 1)
    dot = functools.partial(jnp.dot, preferred_element_type=jnp.float32)

    def step(q, carry):
        taps = [
            [jnp.concatenate([ref[0, q + a], ref[1, q + 2 - a]], axis=1) for a in range(3)] for ref in (high_x, low_x)
        ]
        high, low = taps
        rows = jnp.concatenate([high_w[...], high_w[...], low_w[...]], axis=1)
        total_sum = dot(rows, jnp.concatenate(high + low + high, axis=0))
        for side in range(2):
            lanes = slice(side * across, (side + 1) * across)
            left = pltpu.roll(total_sum[:wide, lanes], 1, 1)
            right = pltpu.roll(total_sum[2 * wide :, lanes], across - 1, 1)
            result = (
                total_sum[wide : 2 * wide, lanes]
                + jnp.where(lane == 0, 0.0, left)
                + jnp.where(lane == across - 1, 0.0, right)
            )
            row = q if side == 0 else outs - 1 - q
            for index, ref in enumerate(results):
                value = result[index * half : (index + 1) * half]
                ref[side, row] = value + sums[index][side, row] if added else value
        return carry

    lax.fori_loop(0, outs, step, 0)


def conv(place, groups, before, weights, pairs, first, last, sums=()):
    arrays, numbers = [], []
    for group in groups:
        numbers.append(tuple(range(len(arrays), len(arrays) + len(group))))
        arrays += group
    channels, across = arrays[0].shape[1:]
    depth = channels * len(groups)
    wide = weights[0].shape[0] // 3
    rows = (1 if first else 2) + pairs + (1 if last else 0)
    outs = rows - 2
    result = jax.ShapeDtypeStruct((2, outs, wide // 2, across), jnp.float32)
    tail = jax.ShapeDtypeStruct((2, 2, 2, depth, across), jnp.bfloat16)
    vmem = pl.BlockSpec(memory_space=pltpu.VMEM)
    flops = 2 * 2 * outs * across * 9 * depth * wide * 3
    return pl.pallas_call(
        functools.partial(conv_kernel, tuple(numbers), pairs, first, last, bool(sums)),
        out_shape=(result, result, tail),
        in_specs=[pl.BlockSpec(memory_space=pltpu.SMEM)] + [vmem] * (len(arrays) + 3 + len(sums)),
        out_specs=(vmem, vmem, vmem),
        scratch_shapes=[
            pltpu.VMEM((2, rows, depth, across), jnp.bfloat16),
            pltpu.VMEM((2, rows, depth, across), jnp.bfloat16),
        ],
        compiler_params=pltpu.CompilerParams(vmem_limit_bytes=VMEM_BYTES),
        cost_estimate=pl.CostEstimate(flops=1000 + int(flops * FACTOR), bytes_accessed=1000, transcendentals=0),
    )(place, *arrays, before, *weights, *sums)


class Cell:
    def __init__(self, value):
        self.value = value


def after(value, cells):
    cells = [cell for cell in cells if cell is not None]
    if not cells:
        return value
    value, *others = lax.optimization_barrier((value, *(cell.value for cell in cells)))
    for cell, other in zip(cells, others):
        cell.value = other
    return value


class Lane:
    def __init__(self, axis, most=2):
        self.axis, self.most, self.sent = axis, most, []

    def send(self, value, pairs, *cells):
        held = self.sent[-self.most] if len(self.sent) >= self.most else None
        cell = Cell(lax.ppermute(after(value, (held,) + cells), self.axis, pairs))
        self.sent.append(cell)
        return cell


def edges(count, step, parity):
    moves = []
    for low in range(parity, count - 1, 2):
        if low >= step:
            moves.append((low, low + 1))
        if low + 1 <= count - 1 - step:
            moves.append((low + 1, low))
    return moves


def gathered_keys(positions):
    keys = [0]
    bit = positions // 2
    while bit:
        keys += [key ^ bit for key in keys]
        bit //= 2
    return keys


def gathered(piece, lane):
    count = lax.axis_size("pos")
    pieces = {0: Cell(piece)}
    bit = count // 2
    while bit:
        swap = [(i, i ^ bit) for i in range(count)]
        pieces.update({key ^ bit: lane.send(cell.value, swap) for key, cell in list(pieces.items())})
        bit //= 2
    return [pieces[key] for key in gathered_keys(count)]


def chunk_sizes(half):
    total = sum(SHARES)
    return [half * share // total for share in SHARES] if half % total == 0 else [half]


ORDER = (
    ("E00",), ("O00",), ("E10",), ("O01",), ("E01",), ("O10",), ("E02",), ("O11",), ("E11",), ("O20", "X2"),
    ("P", "X3"), ("E20",), ("O21",), ("H",), ("E12", "H"), ("O30",), ("A0",), ("E21", "A0"), ("E30", "E12"), ("O31",),
    ("A1",), ("G",), ("E22", "A1"), ("B0", "A0"), ("E31",), ("A2",), ("B1",), ("E32",), ("A3",), ("B2",), ("B3",),
)


def body(activations, filters):
    count, positions = lax.axis_size("filt"), lax.axis_size("pos")
    me, position, layer = lax.axis_index("filt"), lax.axis_index("pos"), lax.axis_index("layer")
    height, channels, across = activations.shape
    half = height // 2
    forward = [(i, i + 1) for i in range(positions - 1)]
    backward = [(i + 1, i) for i, _ in forward]
    swap = [(0, 1), (1, 0)]

    sizes = chunk_sizes(half)
    starts = [sum(sizes[:i]) for i in range(len(sizes))]
    chunks = [
        jnp.concatenate([activations[s : s + m], activations[height - s - m : height - s]], axis=0)
        for s, m in zip(starts, sizes)
    ]
    lanes = {"E": Lane("filt", DEPTHS[0]), "O": Lane("filt", DEPTHS[1]), "Y": Lane("layer", DEPTHS[2])}
    by_swaps = positions & (positions - 1) == 0 and filters.shape[1] % 128 == 0
    late = by_swaps and positions == count == 4 and len(sizes) > 1
    turn = 1 - 2 * (me % 2)
    slots = jnp.arange(count)
    place = (slots if late else jnp.mod(me + turn * slots, count)).astype(jnp.int32)
    order = layer.astype(jnp.int32).reshape(1)
    if by_swaps:
        owners = jnp.stack([position ^ key for key in gathered_keys(positions)])
        owners = jnp.mod(turn * (owners - me), count) if late else owners
        order = jnp.concatenate([order, owners.astype(jnp.int32)])
    cells = {}
    first = Cell(chunks[0])
    held = after(filters, [first])
    chunks[0] = first.value
    if by_swaps:
        pieces = gathered(held, Lane("pos", 99))
    else:
        pieces = [Cell(lax.all_gather(held, "pos", axis=1, tiled=True))]
    cells.update({f"X{index}": cell for index, cell in enumerate(pieces)})

    def move(word, waits):
        kind, index, step = word[0], int(word[1]), int(word[2])
        parity = "EO".index(kind)
        source = Cell(chunks[index]) if step == 0 else cells.get("OE"[parity] + f"{index}{step - 1}")
        moves = edges(count, step, parity)
        if moves and source is not None:
            cells[word] = lanes[kind].send(source.value, moves, *waits)

    def groups(index, taken):
        result = []
        for slot in taken:
            words = [f"E{index}{slot - 1}"] + ([f"O{index}{count - 1 - slot}"] if slot >= 2 else [])
            result.append([cells[word].value for word in words if word in cells] if slot else [chunks[index]])
        return result

    def halo(taken):
        parts = groups(0, taken)
        above, below = (
            jnp.stack([sum(array[row] for array in part) for part in parts]) for row in (2 * sizes[0] - 1, 0)
        )
        return Cell(jnp.stack([lax.ppermute(above, "pos", forward), lax.ppermute(below, "pos", backward)]))

    tails, sums = {}, {}

    def compute(kind, index, waits):
        taken = {"A": range(count - 1), "B": [count - 1], "K": range(count)}[kind]
        begin, end = index == 0, index == len(chunks) - 1
        before = cells["G" if kind == "B" else "H"].value if begin else tails[kind, index - 1]
        weights = [cell.value for cell in prepared[2 * (kind == "B") :][:2]]
        extra = [cell.value for cell in sums[index]] if kind == "B" else ()
        before = after(before, waits)
        send, keep, tails[kind, index] = conv(
            place, groups(index, taken), before, weights, sizes[index], begin, end, extra
        )
        sums[index] = [Cell(send), Cell(keep)]
        cells[f"{kind}{index}"] = sums[index][1]
        if kind != "A":
            cells[f"Y{index}"] = lanes["Y"].send(send, swap)

    if late:
        plan = ORDER
    else:
        plan = [("P",)]
        for index in range(len(chunks)):
            for step in range(count - 1):
                plan += [(f"E{index}{step}",)] + ([(f"O{index}{step}",)] if step < count - 2 else [])
        plan += [("H",)] + [(f"K{index}",) for index in range(len(chunks))]
    for word, *names in plan:
        kind = word[0]
        waits = [cells[name] for name in names if name in cells]
        if kind in "EO":
            move(word, waits)
        elif kind == "P":
            arrays = [cell.value for cell in pieces]
            prepared = [Cell(array) for array in prepare(arrays, order, late)]
            cells["P"] = prepared[0]
        elif kind in "HG":
            cells[kind] = halo([count - 1] if kind == "G" else range(count - 1 if late else count))
        else:
            compute(kind, int(word[1]), waits)
    blocks = [jnp.maximum(sums[index][1].value + cells[f"Y{index}"].value, 0.0) for index in range(len(chunks))]
    return jnp.concatenate([block[0] for block in blocks] + [block[1] for block in reversed(blocks)], axis=0)


def solution(mesh):
    in_specs = (P("pos", ("layer", "filt"), None), P(None, ("layer", "pos"), "filt"))
    out_specs = P("pos", ("filt", "layer"), None)
    return jax.shard_map(body, mesh=mesh, in_specs=in_specs, out_specs=out_specs, check_vma=False)
```
